32 devices in a mesh: groups: 2 (over y), ctx: 4 (over z), state: 2 (over x), head: 2 (over core).
Axes of the slice: x: 2, y: 2, z: 4, core: 2. Of those that a mesh axis runs over, the one named last changes fastest.
Arguments:
- x_in: bfloat16 [4096, 4096], P(('groups', 'ctx'), 'head'), parts along dimension 0, may hold values from -6 to 6
- b_in: bfloat16 [4096, 1024], P(('groups', 'ctx'), 'state'), parts along dimension 0, may hold values from -6 to 6
- c_in: bfloat16 [4096, 1024], P(('groups', 'ctx'), 'state'), parts along dimension 0, may hold values from -6 to 6
- z_in: bfloat16 [4096, 4096], P(('groups', 'ctx'), ('head', 'state')), parts along dimension 0, may hold values from -6 to 6
- dt_raw: float32 [4096, 64], P(('groups', 'ctx'), 'head'), parts along dimension 0, may hold values from -5 to 5
- decay_rate: float32 [64], P('head'), may hold values from 0.00012207031 to 0.05, as said below
- d_skip: float32 [64], P('head'), may hold values from 0.5 to 1.5
- conv_x: float32 [4, 4096], P(None, 'head'), may hold values from -3 to 3
- conv_b: float32 [4, 1024], P(None, 'state'), may hold values from -0.3 to 0.3
- conv_c: float32 [4, 1024], P(None, 'state'), may hold values from -0.3 to 0.3
- norm_gain: float32 [4096], P(('head', 'state')), may hold values from 0.5 to 1.5
- w_out: bfloat16 [4096, 4096], P('ctx', ('state', 'head')), may hold values from -0.09375 to 0.09375
Outputs:
- layer_out: bfloat16 [4096, 4096], P(('groups', 'ctx'), ('state', 'head')), parts along dimension 0
The draws below stay inside these ranges and needn't reach their ends.
There are 2 independent parts, one for each index of `groups`. The reference program is written for one: setup_inputs(seed, part) draws one part's arguments, and reference() takes and returns one part's arrays. A program takes and returns all parts, laid end to end along the dimension named above; an argument that names none is the same for every part. Nothing has to cross between parts.
Inputs may be any that keep to these rules, and one draw needn't show every extreme that they name: `decay_rate`: positive decay rate of each head.
All inputs are finite; a program needn't handle non-finite values.
Results may differ from the reference program's by a relative error of at most 0.014.
Values may be sent and summed in bfloat16 or wider, within the bound.
A program may use at most 128 MiB of HBM per device.

```python
import math
import jax
import jax.numpy as jnp
from jax import lax

D = 4096
HEADS = 64
P_SIZE = 64
NSTATE = 1024
SPAN = 256
KW = 4
TOK_DEV = 512
CH = 4096
TOKENS = 2048


def draw_decay_rate(key, part):
    lowest = math.log(0.25 / TOKENS)
    highest = math.log(0.05)
    key_one = jax.random.fold_in(key, 0)
    return jnp.exp(jax.random.uniform(key_one, (HEADS,), jnp.float32, lowest, highest)).astype(jnp.float32)


def draw_dt_raw(key, part):
    key_one, key_two = jax.random.split(jax.random.fold_in(key, 17))
    block_count = TOKENS // TOK_DEV
    offsets = jax.random.uniform(key_one, (block_count, 1, HEADS), jnp.float32, -2.0, 2.0)
    rough = jnp.clip(0.7 * jax.random.normal(key_two, (block_count, TOK_DEV, HEADS), jnp.float32), -3.0, 3.0)
    return (offsets + rough).reshape(TOKENS, HEADS).astype(jnp.float32)


def block_levels(rng, dims, cuts, least, largest):
    gain, own = 1.0, jax.random.fold_in(rng, 6)
    for dim, blocks in cuts:
        steps = jnp.exp(jax.random.uniform(jax.random.fold_in(own, dim), (blocks,), jnp.float32, least / len(cuts), largest / len(cuts)))
        gain = gain * jnp.repeat(steps, dims[dim] // blocks).reshape([-1 if axis == dim else 1 for axis in range(len(dims))])
    return gain


def gaussian(key, dims, deviation, most, cuts=(), dtype=jnp.bfloat16):
    array = jax.random.normal(key, dims, jnp.float32) * deviation
    if len(cuts) > 0:
        array = block_levels(key, dims, cuts, -0.22, 0.18) * array
    return jnp.clip(array, min=-most, max=most).astype(dtype)


def setup_inputs(seed: int = 0, part: int = 0) -> dict:
    streams_of = jax.random.split(jax.random.key(seed), 13)
    part_keys = jax.random.split(jax.random.fold_in(streams_of[12], part), 13)
    x_in = gaussian(part_keys[0], (TOKENS, CH), 1.0, 6.0, ((0, 4), (1, 2)))
    b_in = gaussian(part_keys[1], (TOKENS, NSTATE), 1.0, 6.0, ((0, 4), (1, 2)))
    c_in = gaussian(part_keys[2], (TOKENS, NSTATE), 1.0, 6.0, ((0, 4), (1, 2)))
    z_in = gaussian(part_keys[3], (TOKENS, CH), 1.0, 6.0, ((0, 4), (1, 4)))
    dt_raw = draw_dt_raw(jax.random.fold_in(jax.random.fold_in(streams_of[12], part), 71), part)
    decay_rate = draw_decay_rate(jax.random.fold_in(streams_of[12], 71), part)
    d_skip = jnp.clip(0.5 + 1.0 * jax.random.uniform(streams_of[6], (HEADS,), jnp.float32) ** block_levels(streams_of[6], (HEADS,), ((0, 2),), -0.2, 0.2), 0.5, 1.5)
    conv_x = gaussian(streams_of[7], (KW, CH), 0.5, 3.0, ((1, 2),), jnp.float32)
    conv_b = gaussian(streams_of[8], (KW, NSTATE), 0.05, 0.3, ((1, 2),), jnp.float32)
    conv_c = gaussian(streams_of[9], (KW, NSTATE), 0.05, 0.3, ((1, 2),), jnp.float32)
    norm_gain = jnp.clip(0.5 + 1.0 * jax.random.uniform(streams_of[10], (CH,), jnp.float32) ** block_levels(streams_of[10], (CH,), ((0, 4),), -0.2, 0.2), 0.5, 1.5)
    w_out = gaussian(streams_of[11], (CH, D), CH ** -0.5, 0.09375, ((0, 4), (1, 4)))
    return dict(x_in=x_in, b_in=b_in, c_in=c_in, z_in=z_in, dt_raw=dt_raw, decay_rate=decay_rate, d_skip=d_skip, conv_x=conv_x, conv_b=conv_b, conv_c=conv_c, norm_gain=norm_gain, w_out=w_out)


def conv_silu(signal, before, weights):
    length = signal.shape[0]
    tap_count = weights.shape[0]
    joined = jnp.concatenate([before, signal], axis=0).astype(jnp.float32)
    summed = weights[tap_count - 1] * joined[tap_count - 1:]
    for tap_index in range(tap_count - 1):
        summed = summed + weights[tap_index] * joined[tap_index:tap_index + length]
    return jax.nn.silu(summed).astype(jnp.bfloat16)

def reference(x_in, b_in, c_in, z_in, dt_raw, decay_rate, d_skip, conv_x, conv_b, conv_c, norm_gain, w_out):
    tap_count = conv_x.shape[0]
    x_conv = conv_silu(x_in, jnp.zeros((tap_count - 1, CH), jnp.bfloat16), conv_x)
    b_conv = conv_silu(b_in, jnp.zeros((tap_count - 1, NSTATE), jnp.bfloat16), conv_b)
    c_conv = conv_silu(c_in, jnp.zeros((tap_count - 1, NSTATE), jnp.bfloat16), conv_c)
    span_count = TOKENS // SPAN
    step_size = jax.nn.softplus(dt_raw).reshape(span_count, SPAN, HEADS)
    x_blocks = x_conv.reshape(span_count, SPAN, HEADS, P_SIZE)
    b_blocks = b_conv.reshape(span_count, SPAN, NSTATE)
    c_blocks = c_conv.reshape(span_count, SPAN, NSTATE)
    causal = jnp.arange(SPAN)[:, None] >= jnp.arange(SPAN)[None, :]
    highest = lax.Precision.HIGHEST

    def one_span(state_now, pieces):
        x_piece, b_piece, c_piece, step_piece = pieces
        cumulative = jnp.cumsum(-decay_rate * step_piece, axis=0)
        span_total = cumulative[-1]
        x_float = x_piece.astype(jnp.float32)
        inner_all = jnp.dot(c_piece, b_piece.T, preferred_element_type=jnp.float32)
        cum_heads = cumulative.T
        log_gap = cum_heads[:, :, None] - cum_heads[:, None, :]
        scores = (inner_all[None] * jnp.exp(jnp.where(causal, log_gap, -jnp.inf))).astype(jnp.bfloat16)
        scores = lax.optimization_barrier(scores)
        inputs = (step_piece[:, :, None] * x_float).astype(jnp.bfloat16)
        inputs = lax.optimization_barrier(inputs)
        intra = jnp.einsum('hts,shp->thp', scores.astype(jnp.float32), inputs.astype(jnp.float32), precision=highest)
        states_b = lax.optimization_barrier(state_now.astype(jnp.bfloat16))
        inter = jnp.einsum('tn,hpn->thp', c_piece.astype(jnp.float32), states_b.astype(jnp.float32), precision=highest)
        inter = inter * jnp.exp(cumulative)[:, :, None]
        weighted = ((jnp.exp(span_total[None] - cumulative) * step_piece)[:, :, None] * x_float).astype(jnp.bfloat16)
        weighted = lax.optimization_barrier(weighted)
        update = jnp.einsum('thp,tn->hpn', weighted.astype(jnp.float32), b_piece.astype(jnp.float32), precision=highest)
        state_next = jnp.exp(span_total)[:, None, None] * state_now + update
        result = intra + d_skip[None, :, None] * x_float + inter
        return (state_next, result)
    start_state = jnp.zeros((HEADS, P_SIZE, NSTATE), jnp.float32)
    final_state, outputs = lax.scan(one_span, start_state, (x_blocks, b_blocks, c_blocks, step_size))
    mixed = outputs.reshape(TOKENS, CH)
    gated = mixed * jax.nn.silu(z_in.astype(jnp.float32))
    mean_square = lax.optimization_barrier(jnp.sum(gated * gated, axis=1)) / CH
    normed = (gated * lax.rsqrt(mean_square + 1e-05)[:, None] * norm_gain).astype(jnp.bfloat16)
    return jnp.dot(normed, w_out, preferred_element_type=jnp.float32).astype(jnp.bfloat16)
```

```python
import jax
import jax.numpy as jnp
from jax import lax
from jax.sharding import PartitionSpec as P

SPAN = 256
CHUNKS = 4


def conv_silu(signal, before, weights):
    length = signal.shape[0]
    taps = weights.shape[0]
    joined = jnp.concatenate([before, signal], axis=0).astype(jnp.float32)
    summed = weights[taps - 1] * joined[taps - 1 :]
    for k in range(taps - 1):
        summed = summed + weights[k] * joined[k : k + length]
    return jax.nn.silu(summed).astype(jnp.bfloat16)


def local(
    x_in, b_in, c_in, z_in, dt_raw, decay_rate, d_skip, conv_x, conv_b, conv_c, norm_gain, w_out
):
    f32, bf16 = jnp.float32, jnp.bfloat16
    parts = lax.axis_size("state")
    part = lax.axis_index("state")
    ctx = lax.axis_size("ctx")
    me = lax.axis_index("ctx")
    groups = lax.axis_size("groups")
    tokens = x_in.shape[0]
    heads = dt_raw.shape[1] // parts
    width = x_in.shape[1] // parts
    size = width // heads
    nb = b_in.shape[1]
    taps = conv_x.shape[0]
    spans = tokens // SPAN
    total_channels = width * parts * lax.axis_size("head")

    rows = w_out.shape[0] // groups
    w_half = lax.dynamic_slice_in_dim(w_out, lax.axis_index("groups") * rows, rows, 0)
    w_all = lax.all_gather(w_half, ("ctx", "groups"), axis=0, tiled=True)

    own = lambda a, axis: lax.dynamic_slice_in_dim(
        a, part * (a.shape[axis] // parts), a.shape[axis] // parts, axis
    )
    x_own, dt_own, rate, skip, taps_x = (
        own(x_in, 1), own(dt_raw, 1), own(decay_rate, 0), own(d_skip, 0), own(conv_x, 1)
    )
    rim = tokens - (taps - 1)
    packed = jnp.concatenate([x_own[rim:], b_in[rim:], c_in[rim:]], axis=1)
    onward = [(i, i + 1) for i in range(ctx - 1)]
    arrived = lax.ppermute(packed, "ctx", onward)
    bc = conv_silu(
        jnp.concatenate([b_in, c_in], axis=1),
        arrived[:, width:],
        jnp.concatenate([conv_b, conv_c], axis=1),
    )
    bc_all = lax.all_gather(bc, "state", axis=0)
    x_conv = conv_silu(x_own, arrived[:, :width], taps_x)
    b = jnp.concatenate([bc_all[i, :, :nb] for i in range(parts)], axis=1)
    c = jnp.concatenate([bc_all[i, :, nb:] for i in range(parts)], axis=1)
    b = b.reshape(spans, SPAN, parts * nb)
    c = c.reshape(spans, SPAN, parts * nb)
    step = jax.nn.softplus(dt_own).reshape(spans, SPAN, heads)
    causal = jnp.arange(SPAN)[:, None] >= jnp.arange(SPAN)[None, :]
    cum = jnp.einsum(
        "ts,ksh->kth", causal.astype(f32), -rate * step, precision=lax.Precision.HIGHEST
    )
    last = cum[:, -1, :]
    x_heads = x_conv.reshape(spans, SPAN, heads, size).astype(f32)
    weighted = ((jnp.exp(last[:, None, :] - cum) * step)[..., None] * x_heads).astype(bf16)
    update = jnp.einsum("kthp,ktn->khpn", weighted, b, preferred_element_type=f32)
    running = jnp.zeros_like(update[0])
    entering, reach, gain = [], [], jnp.ones_like(last[0])
    for k in range(spans):
        entering.append(running)
        reach.append(gain)
        decay = jnp.exp(last[k])
        running = decay[:, None, None] * running + update[k]
        gain = gain * decay
    some = heads // CHUNKS
    final = running.reshape(CHUNKS, some, size, -1)
    gain_c = gain.reshape(CHUNKS, some)
    prior = jnp.zeros(final.shape, bf16)
    got = jnp.zeros(final.shape[1:], bf16)
    for t in range(CHUNKS + ctx - 1):
        place = jnp.clip(t - me, 0, CHUNKS - 1)
        fits = (t >= me) & (t - me < CHUNKS)
        if t > 0:
            old = lax.dynamic_index_in_dim(prior, place, 0, keepdims=False)
            prior = lax.dynamic_update_index_in_dim(prior, jnp.where(fits, got, old), place, 0)
        if t < CHUNKS + ctx - 2:
            mine = lax.dynamic_index_in_dim(final, place, 0, keepdims=False)
            factor = lax.dynamic_index_in_dim(gain_c, place, 0, keepdims=False)
            send = (factor[:, None, None] * got.astype(f32) + mine).astype(bf16)
            got = lax.ppermute(send, "ctx", onward)
    prior = prior.reshape(running.shape).astype(f32)

    inner = jnp.einsum("ktn,ksn->kts", c, b, preferred_element_type=f32)
    cum_heads = jnp.transpose(cum, (0, 2, 1))
    gap = cum_heads[:, :, :, None] - cum_heads[:, :, None, :]
    scores = (inner[:, None] * jnp.exp(jnp.where(causal, gap, -jnp.inf))).astype(bf16)
    inputs = (step[..., None] * x_heads).astype(bf16)
    intra = jnp.einsum("khts,kshp->kthp", scores, inputs, preferred_element_type=f32)
    states = (jnp.stack(reach)[:, :, None, None] * prior + jnp.stack(entering)).astype(bf16)
    inter = jnp.einsum("ktn,khpn->kthp", c, states, preferred_element_type=f32)
    mixed = intra + skip[:, None] * x_heads + jnp.exp(cum)[..., None] * inter
    gated = mixed.reshape(tokens, width) * jax.nn.silu(z_in.astype(f32))
    square = lax.psum(jnp.sum(gated * gated, axis=1), ("state", "head"))
    everything = lax.all_gather(
        (gated * norm_gain).astype(bf16), ("head", "state"), axis=1, tiled=True
    )
    result = jnp.dot(everything, w_all, preferred_element_type=f32)
    result = result * lax.rsqrt(square / total_channels + 1e-05)[:, None]
    return result.astype(bf16)


def solution(mesh):
    return jax.shard_map(
        local,
        mesh=mesh,
        in_specs=(
            P(("groups", "ctx"), "head"),
            P(("groups", "ctx"), "state"),
            P(("groups", "ctx"), "state"),
            P(("groups", "ctx"), ("head", "state")),
            P(("groups", "ctx"), "head"),
            P("head"),
            P("head"),
            P(None, "head"),
            P(None, "state"),
            P(None, "state"),
            P(("head", "state")),
            P("ctx", ("state", "head")),
        ),
        out_specs=P(("groups", "ctx"), ("state", "head")),
        check_vma=False,
    )
```

```python
import functools

import jax
import jax.numpy as jnp
from jax import lax
from jax.experimental import pallas as pl
from jax.experimental.pallas import tpu as pltpu
from jax.sharding import PartitionSpec as P

SPAN = 256
CHUNK = 256


def conv_silu(signal, before, weights):
    length = signal.shape[0]
    taps = weights.shape[0]
    joined = jnp.concatenate([before, signal], axis=0).astype(jnp.float32)
    summed = weights[taps - 1] * joined[taps - 1 :]
    for k in range(taps - 1):
        summed = summed + weights[k] * joined[k : k + length]
    return jax.nn.silu(summed).astype(jnp.bfloat16)


def kernel(
    axes, w_ref, final_ref, factor_ref, reach_ref, entering_ref, c_ref, base_ref, grow_ref, z_ref,
    gain_ref, o_ref, w_all, prior, outgoing, gates, squares, total,
    wr_send, wr_recv, wl_send, wl_recv, wy_send, wy_recv, st_send, st_recv,
    gx_send, gx_recv, gc_send, gc_recv, sq_send, sq_recv,
):
    f32, bf16 = jnp.float32, jnp.bfloat16
    G, C, S, H = axes
    g, me, s, h = (lax.axis_index(a) for a in ("groups", "ctx", "state", "head"))
    rows = w_ref.shape[0]
    part = rows // G
    K, nstate, cw = prior.shape
    tokens = c_ref.shape[0]
    spans = tokens // SPAN
    remote = functools.partial(
        pltpu.make_async_remote_copy, device_id_type=pl.DeviceIdType.MESH
    )

    others = [(a, b) for a in range(H) for b in range(S) if a or b]
    barrier = pltpu.get_barrier_semaphore()

    def greet(to):
        pl.semaphore_signal(barrier, inc=1, device_id=to, device_id_type=pl.DeviceIdType.MESH)

    pl.when(me > 0)(lambda: greet({"ctx": me - 1}))
    pl.when(me < C - 1)(lambda: greet({"ctx": me + 1}))
    for a in range(1, G):
        greet({"groups": lax.rem(g + a, G)})
    for a, b in others:
        greet({"head": lax.rem(h + a, H), "state": lax.rem(s + b, S)})
    peers = G - 1 + len(others) + (me > 0).astype(jnp.int32) + (me < C - 1).astype(jnp.int32)
    pl.semaphore_wait(barrier, peers)

    def piece(j, half):
        return w_all.at[pl.ds(pl.multiple_of(j * rows + half * part, part), part)]

    def right(k, j):
        return remote(piece(j, g), piece(j, g), wr_send.at[k], wr_recv.at[k], device_id={"ctx": me + 1})

    def left(k, j):
        return remote(piece(j, g), piece(j, g), wl_send.at[k], wl_recv.at[k], device_id={"ctx": me - 1})

    def across(way, k, a, j, half):
        return remote(
            piece(j, half), piece(j, half), wy_send.at[way, k, a - 1], wy_recv.at[way, k, a - 1],
            device_id={"groups": lax.rem(g + a, G)},
        )

    def weights_step(k):
        @pl.when(me - 1 - k >= 0)
        def _():
            right(k, me - 1 - k).wait_recv()
            for a in range(1, G):
                across(0, k, a, me - 1 - k, g).start()
            if k + 1 <= C - 2:
                pl.when(me < C - 1)(lambda: right(k + 1, me - 1 - k).start())

        @pl.when(me + 1 + k <= C - 1)
        def _():
            left(k, me + 1 + k).wait_recv()
            for a in range(1, G):
                across(1, k, a, me + 1 + k, g).start()
            if k + 1 <= C - 2:
                pl.when(me > 0)(lambda: left(k + 1, me + 1 + k).start())

    def weights_end(k):
        @pl.when((me - k >= 0) & (me < C - 1))
        def _():
            right(k, me - k).wait_send()

        @pl.when((me + k <= C - 1) & (me > 0))
        def _():
            left(k, me + k).wait_send()

        for way, j, there in ((0, me - 1 - k, me - 1 - k >= 0), (1, me + 1 + k, me + 1 + k <= C - 1)):
            @pl.when(there)
            def _():
                for a in range(1, G):
                    across(way, k, a, j, g).wait_send()
                    across(way, k, a, j, lax.rem(g - a + G, G)).wait_recv()

    def state(q):
        return remote(
            outgoing.at[q], prior.at[q], st_send.at[q], st_recv.at[q], device_id={"ctx": me + 1}
        )

    def block(a, b, q):
        return (lax.rem(h + H - a, H) * S + lax.rem(s + S - b, S)) * K + q

    def gate_x(b, q, blk):
        return remote(
            gates.at[blk], gates.at[blk], gx_send.at[b - 1, q], gx_recv.at[b - 1, q],
            device_id={"state": lax.rem(s + b, S)},
        )

    def gate_core(a, b, q, blk):
        return remote(
            gates.at[blk], gates.at[blk], gc_send.at[a - 1, b, q], gc_recv.at[a - 1, b, q],
            device_id={"head": lax.rem(h + a, H)},
        )

    def square(i, slot):
        a, b = others[i]
        return remote(
            squares.at[slot], squares.at[slot], sq_send.at[i], sq_recv.at[i],
            device_id={"head": lax.rem(h + a, H), "state": lax.rem(s + b, S)},
        )

    w_all[pl.ds(pl.multiple_of(me * rows, rows), rows)] = w_ref[...]

    pl.when(me < C - 1)(lambda: right(0, me).start())
    pl.when(me > 0)(lambda: left(0, me).start())

    @pl.when(me == 0)
    def _():
        prior[...] = jnp.zeros_like(prior)

    summed = jnp.zeros((tokens, 1), f32)
    for q in range(K):
        cols = slice(q * cw, (q + 1) * cw)
        pl.when(me > 0)(lambda: state(q).wait_recv())

        @pl.when(me < C - 1)
        def _():
            outgoing[q] = (
                factor_ref[:, cols] * prior[q].astype(f32) + final_ref[:, cols]
            ).astype(bf16)
            state(q).start()

        own = block(0, 0, q)
        parts = []
        for k in range(spans):
            t = slice(k * SPAN, (k + 1) * SPAN)
            there = reach_ref[k : k + 1, cols] * prior[q].astype(f32)
            if k > 0:
                there = there + entering_ref[k - 1, :, cols]
            inter = jnp.dot(c_ref[t, :], there.astype(bf16), preferred_element_type=f32)
            mixed = base_ref[t, cols] + grow_ref[t, cols] * inter
            z = z_ref[t, cols].astype(f32)
            gated = mixed * (z / (1.0 + jnp.exp(-z)))
            parts.append(jnp.sum(gated * gated, axis=1, keepdims=True))
            gates[own, t, :] = (gated * gain_ref[:, cols]).astype(bf16)
        summed = summed + jnp.concatenate(parts, axis=0)
        for b in range(1, S):
            gate_x(b, q, own).start()
        for a in range(1, H):
            gate_core(a, 0, q, own).start()
        if 1 <= q <= C - 1:
            weights_step(q - 1)
    here = h * S + s
    squares[here] = jnp.broadcast_to(summed, (tokens, 128)).T[:8]
    for i in range(len(others)):
        square(i, here).start()
    for k in range(min(K - 1, C - 1), C - 1):
        weights_step(k)
    for q in range(K):
        for b in range(1, S):
            gate_x(b, q, block(0, b, q)).wait_recv()
            for a in range(1, H):
                gate_core(a, b, q, block(0, b, q)).start()
    for q in range(K):
        for a in range(1, H):
            for b in range(S):
                gate_core(a, b, q, block(a, b, q)).wait_recv()
    for k in range(C - 1):
        weights_end(k)
    for i, (a, b) in enumerate(others):
        square(i, block(a, b, 0) // K).wait_recv()
    mean = jnp.sum(squares[...], axis=0)[:1] / (S * H * K * cw)
    scale = lax.rsqrt(jnp.broadcast_to(mean + 1e-05, (128, tokens)).T[:, :1])
    total[...] = jnp.zeros_like(total)

    @pl.loop(0, S * H * K)
    def _(blk):
        total[...] += jnp.dot(
            gates[blk], w_all[pl.ds(pl.multiple_of(blk * cw, cw), cw)], preferred_element_type=f32
        )

    o_ref[...] = (total[...] * scale).astype(bf16)
    pl.when(me < C - 1)(lambda: [state(q).wait_send() for q in range(K)] and None)
    for q in range(K):
        for b in range(1, S):
            gate_x(b, q, block(0, 0, q)).wait_send()
        for a in range(1, H):
            for b in range(S):
                gate_core(a, b, q, block(0, b, q)).wait_send()
    for i in range(len(others)):
        square(i, here).wait_send()


def finish(axes, w, final, factor, reach, entering, c, base, grow, z, gain):
    G, C, S, H = axes
    bf16, f32 = jnp.bfloat16, jnp.float32
    nstate, width = final.shape
    tokens = c.shape[0]
    cw = min(CHUNK, width)
    K = width // cw
    dma = pltpu.SemaphoreType.DMA
    args = (w, final, factor, reach, entering, c, base, grow, z, gain)
    return pl.pallas_call(
        functools.partial(kernel, axes),
        out_shape=jax.ShapeDtypeStruct((tokens, w.shape[1]), bf16),
        in_specs=[pl.BlockSpec(memory_space=pltpu.VMEM)] * len(args),
        out_specs=pl.BlockSpec(memory_space=pltpu.VMEM),
        scratch_shapes=[
            pltpu.VMEM((C * w.shape[0], w.shape[1]), bf16),
            pltpu.VMEM((K, nstate, cw), bf16),
            pltpu.VMEM((K, nstate, cw), bf16),
            pltpu.VMEM((S * H * K, tokens, cw), bf16),
            pltpu.VMEM((S * H, 8, tokens), f32),
            pltpu.VMEM((tokens, w.shape[1]), f32),
            dma((C - 1,)), dma((C - 1,)), dma((C - 1,)), dma((C - 1,)),
            dma((2, C - 1, G - 1)), dma((2, C - 1, G - 1)), dma((K,)), dma((K,)),
            dma((S - 1, K)), dma((S - 1, K)), dma((H - 1, S, K)), dma((H - 1, S, K)),
            dma((S * H - 1,)), dma((S * H - 1,)),
        ],
        compiler_params=pltpu.CompilerParams(
            collective_id=0, has_side_effects=True, vmem_limit_bytes=60 * 2**20
        ),
    )(*args)


def local(
    x_in, b_in, c_in, z_in, dt_raw, decay_rate, d_skip, conv_x, conv_b, conv_c, norm_gain, w_out
):
    f32, bf16 = jnp.float32, jnp.bfloat16
    parts = lax.axis_size("state")
    part = lax.axis_index("state")
    ctx = lax.axis_size("ctx")
    groups = lax.axis_size("groups")
    tokens = x_in.shape[0]
    heads = dt_raw.shape[1] // parts
    width = x_in.shape[1] // parts
    size = width // heads
    nb = b_in.shape[1]
    taps = conv_x.shape[0]
    spans = tokens // SPAN
    own = lambda a, axis: lax.dynamic_slice_in_dim(
        a, part * (a.shape[axis] // parts), a.shape[axis] // parts, axis
    )
    x_own, dt_own, rate, skip, taps_x = (
        own(x_in, 1), own(dt_raw, 1), own(decay_rate, 0), own(d_skip, 0), own(conv_x, 1)
    )
    rim = tokens - (taps - 1)
    packed = jnp.concatenate([x_own[rim:], b_in[rim:], c_in[rim:]], axis=1)
    onward = [(i, i + 1) for i in range(ctx - 1)]
    arrived = lax.ppermute(packed, "ctx", onward)
    bc = conv_silu(
        jnp.concatenate([b_in, c_in], axis=1),
        arrived[:, width:],
        jnp.concatenate([conv_b, conv_c], axis=1),
    )
    bc_all = lax.all_gather(bc, "state", axis=0)
    x_conv = conv_silu(x_own, arrived[:, :width], taps_x)
    b = jnp.concatenate([bc_all[i, :, :nb] for i in range(parts)], axis=1)
    c = jnp.concatenate([bc_all[i, :, nb:] for i in range(parts)], axis=1)
    b = b.reshape(spans, SPAN, parts * nb)
    c = c.reshape(spans, SPAN, parts * nb)
    step = jax.nn.softplus(dt_own).reshape(spans, SPAN, heads)
    causal = jnp.arange(SPAN)[:, None] >= jnp.arange(SPAN)[None, :]
    cum = jnp.einsum(
        "ts,ksh->kth", causal.astype(f32), -rate * step, precision=lax.Precision.HIGHEST
    )
    last = cum[:, -1, :]
    x_heads = x_conv.reshape(spans, SPAN, heads, size).astype(f32)
    weighted = ((jnp.exp(last[:, None, :] - cum) * step)[..., None] * x_heads).astype(bf16)
    wide = lambda v: jnp.repeat(v, size, axis=-1)
    weighted = weighted.reshape(spans, SPAN, width)
    update = jnp.einsum("ktn,ktm->knm", b, weighted, preferred_element_type=f32)
    running = update[0]
    gain = jnp.exp(last[0])
    entering, reach = [], [jnp.ones_like(gain)]
    for k in range(1, spans):
        entering.append(running)
        reach.append(gain)
        decay = jnp.exp(last[k])
        running = wide(decay) * running + update[k]
        gain = gain * decay
    inner = jnp.einsum("ktn,ksn->kts", c, b, preferred_element_type=f32)
    cum_heads = jnp.transpose(cum, (0, 2, 1))
    gap = cum_heads[:, :, :, None] - cum_heads[:, :, None, :]
    scores = (inner[:, None] * jnp.exp(jnp.where(causal, gap, -jnp.inf))).astype(bf16)
    inputs = (step[..., None] * x_heads).astype(bf16)
    intra = jnp.einsum("khts,kshp->kthp", scores, inputs, preferred_element_type=f32)
    base = (intra + skip[:, None] * x_heads).reshape(tokens, width)
    return finish(
        (groups, ctx, parts, lax.axis_size("head")),
        w_out,
        running,
        wide(gain)[None],
        wide(jnp.stack(reach)),
        jnp.stack(entering),
        c.reshape(tokens, -1),
        base,
        wide(jnp.exp(cum)).reshape(tokens, width),
        z_in,
        norm_gain[None],
    )


def solution(mesh):
    return jax.shard_map(
        local,
        mesh=mesh,
        in_specs=(
            P(("groups", "ctx"), "head"),
            P(("groups", "ctx"), "state"),
            P(("groups", "ctx"), "state"),
            P(("groups", "ctx"), ("head", "state")),
            P(("groups", "ctx"), "head"),
            P("head"),
            P("head"),
            P(None, "head"),
            P(None, "state"),
            P(None, "state"),
            P(("head", "state")),
            P("ctx", ("state", "head")),
        ),
        out_specs=P(("groups", "ctx"), ("state", "head")),
        check_vma=False,
    )
```

```python
import functools

import jax
import jax.numpy as jnp
from jax import lax
from jax.experimental import pallas as pl
from jax.experimental.pallas import tpu as pltpu
from jax.sharding import PartitionSpec as P

SPAN = 256
CHUNK = 256
LANES = 128
RIM = 16


def kernel(
    axes, w_ref, x_ref, b_ref, c_ref, z_ref, stepw_ref, cumw_ref, cum_ref, cumt_ref, skip_ref,
    tx_ref, tb_ref, tc_ref, gain_ref, o_ref, w_all, prior, outgoing, gates, squares, total,
    rims, joined, x_conv, bc, inner, rim_send, rim_recv, bx_send, bx_recv, bh_send, bh_recv,
    wr_send, wr_recv, wl_send, wl_recv, wy_send, wy_recv, st_send, st_recv,
    gx_send, gx_recv, gc_send, gc_recv, sq_send, sq_recv,
):
    f32, bf16 = jnp.float32, jnp.bfloat16
    G, C, S, H = axes
    g, me, s, h = (lax.axis_index(a) for a in ("groups", "ctx", "state", "head"))
    rows = w_ref.shape[0]
    part = rows // G
    K, nstate, cw = prior.shape
    tokens, nb = c_ref.shape
    width = x_ref.shape[1]
    size = width // cum_ref.shape[1]
    spans = tokens // SPAN
    remote = functools.partial(
        pltpu.make_async_remote_copy, device_id_type=pl.DeviceIdType.MESH
    )

    others = [(a, b) for a in range(H) for b in range(S) if a or b]
    barrier = pltpu.get_barrier_semaphore()

    def greet(to):
        pl.semaphore_signal(barrier, inc=1, device_id=to, device_id_type=pl.DeviceIdType.MESH)

    pl.when(me > 0)(lambda: greet({"ctx": me - 1}))
    pl.when(me < C - 1)(lambda: greet({"ctx": me + 1}))
    for a in range(1, G):
        greet({"groups": lax.rem(g + a, G)})
    for a, b in others:
        greet({"head": lax.rem(h + a, H), "state": lax.rem(s + b, S)})
    peers = G - 1 + len(others) + (me > 0).astype(jnp.int32) + (me < C - 1).astype(jnp.int32)
    pl.semaphore_wait(barrier, peers)

    def piece(j, half):
        return w_all.at[pl.ds(pl.multiple_of(j * rows + half * part, part), part)]

    def right(k, j):
        return remote(piece(j, g), piece(j, g), wr_send.at[k], wr_recv.at[k], device_id={"ctx": me + 1})

    def left(k, j):
        return remote(piece(j, g), piece(j, g), wl_send.at[k], wl_recv.at[k], device_id={"ctx": me - 1})

    def across(way, k, a, j, half):
        return remote(
            piece(j, half), piece(j, half), wy_send.at[way, k, a - 1], wy_recv.at[way, k, a - 1],
            device_id={"groups": lax.rem(g + a, G)},
        )

    def weights_step(k):
        @pl.when(me - 1 - k >= 0)
        def _():
            right(k, me - 1 - k).wait_recv()
            for a in range(1, G):
                across(0, k, a, me - 1 - k, g).start()
            if k + 1 <= C - 2:
                pl.when(me < C - 1)(lambda: right(k + 1, me - 1 - k).start())

        @pl.when(me + 1 + k <= C - 1)
        def _():
            left(k, me + 1 + k).wait_recv()
            for a in range(1, G):
                across(1, k, a, me + 1 + k, g).start()
            if k + 1 <= C - 2:
                pl.when(me > 0)(lambda: left(k + 1, me + 1 + k).start())

    def weights_end(k):
        @pl.when((me - k >= 0) & (me < C - 1))
        def _():
            right(k, me - k).wait_send()

        @pl.when((me + k <= C - 1) & (me > 0))
        def _():
            left(k, me + k).wait_send()

        for way, j, there in ((0, me - 1 - k, me - 1 - k >= 0), (1, me + 1 + k, me + 1 + k <= C - 1)):
            @pl.when(there)
            def _():
                for a in range(1, G):
                    across(way, k, a, j, g).wait_send()
                    across(way, k, a, j, lax.rem(g - a + G, G)).wait_recv()

    def state(q):
        return remote(
            outgoing.at[q], prior.at[q], st_send.at[q], st_recv.at[q], device_id={"ctx": me + 1}
        )

    def block(a, b, q):
        return (lax.rem(h + H - a, H) * S + lax.rem(s + S - b, S)) * K + q

    def gate_x(b, q, blk):
        return remote(
            gates.at[blk], gates.at[blk], gx_send.at[b - 1, q], gx_recv.at[b - 1, q],
            device_id={"state": lax.rem(s + b, S)},
        )

    def gate_core(a, b, q, blk):
        return remote(
            gates.at[blk], gates.at[blk], gc_send.at[a - 1, b, q], gc_recv.at[a - 1, b, q],
            device_id={"head": lax.rem(h + a, H)},
        )

    def square(i, slot):
        a, b = others[i]
        return remote(
            squares.at[slot], squares.at[slot], sq_send.at[i], sq_recv.at[i],
            device_id={"head": lax.rem(h + a, H), "state": lax.rem(s + b, S)},
        )

    def rim(i):
        ref, at = ((x_ref, 0), (b_ref, width), (c_ref, width + nb))[i]
        return remote(
            ref.at[pl.ds(tokens - RIM, RIM)], rims.at[:, pl.ds(at, ref.shape[1])],
            rim_send.at[i], rim_recv.at[i], device_id={"ctx": me + 1},
        )

    def half_x(b):
        return remote(
            bc.at[h, s], bc.at[h, s], bx_send.at[b - 1], bx_recv.at[b - 1],
            device_id={"state": lax.rem(s + b, S)},
        )

    def half_core(b, which):
        there = lax.rem(s + S - b, S)
        return remote(
            bc.at[which, there], bc.at[which, there], bh_send.at[b - 1], bh_recv.at[b - 1],
            device_id={"head": 1 - h},
        )

    for i in range(3):
        pl.when(me < C - 1)(lambda: rim(i).start())
    w_all[pl.ds(pl.multiple_of(me * rows, rows), rows)] = w_ref[...]

    pl.when(me < C - 1)(lambda: right(0, me).start())
    pl.when(me > 0)(lambda: left(0, me).start())

    @pl.when(me == 0)
    def _():
        prior[...] = jnp.zeros_like(prior)
        rims[...] = jnp.zeros_like(rims)

    for i in range(3):
        pl.when(me > 0)(lambda: rim(i).wait_recv())

    def conv(ref, taps_ref, at):
        wide = ref.shape[1]
        joined[:RIM, :wide] = rims[:, at : at + wide].astype(f32)
        joined[RIM:, :wide] = ref[...].astype(f32)
        taps = taps_ref.shape[0]
        v = jnp.zeros((tokens, wide), f32)
        for k in range(taps):
            v = v + taps_ref[k : k + 1, :] * joined[pl.ds(RIM - taps + 1 + k, tokens), :wide]
        return (v / (1.0 + jnp.exp(-v))).astype(bf16)

    bc[0, s] = conv(b_ref, tb_ref, width)
    bc[1, s] = conv(c_ref, tc_ref, width + nb)
    for b in range(1, S):
        half_x(b).start()
    x_conv[...] = conv(x_ref, tx_ref, 0)
    for b in range(1, S):
        half_x(b).wait_recv()
        half_core(b, h).start()
    for b in range(1, S):
        half_core(b, 1 - h).wait_recv()
    causal = lax.broadcasted_iota(jnp.int32, (SPAN, SPAN), 0) >= lax.broadcasted_iota(
        jnp.int32, (SPAN, SPAN), 1
    )
    lane = lax.broadcasted_iota(jnp.int32, (SPAN, LANES), 1) // size
    for k in range(spans):
        t = slice(k * SPAN, (k + 1) * SPAN)
        inner[k] = sum(
            lax.dot_general(
                bc[1, b, t, :], bc[0, b, t, :], (((1,), (1,)), ((), ())), preferred_element_type=f32
            )
            for b in range(S)
        )

    summed = jnp.zeros((tokens, 1), f32)
    for q in range(K):
        cols = slice(q * cw, (q + 1) * cw)
        running = jnp.zeros((nstate, cw), f32)
        reach = jnp.ones((1, cw), f32)
        before = []
        for k in range(spans):
            t = slice(k * SPAN, (k + 1) * SPAN)
            before.append((reach, running))
            last = cumw_ref[(k + 1) * SPAN - 1 : (k + 1) * SPAN, cols]
            weighted = (
                jnp.exp(last - cumw_ref[t, cols]) * stepw_ref[t, cols] * x_conv[t, cols].astype(f32)
            ).astype(bf16)
            update = jnp.concatenate(
                [
                    lax.dot_general(
                        bc[0, b, t, :], weighted, (((0,), (0,)), ((), ())), preferred_element_type=f32
                    )
                    for b in range(S)
                ],
                axis=0,
            )
            decay = jnp.exp(last)
            running = decay * running + update
            reach = reach * decay
        pl.when(me > 0)(lambda: state(q).wait_recv())

        @pl.when(me < C - 1)
        def _():
            outgoing[q] = (reach * prior[q].astype(f32) + running).astype(bf16)
            state(q).start()

        own = block(0, 0, q)
        parts = []
        for k in range(spans):
            t = slice(k * SPAN, (k + 1) * SPAN)
            x = x_conv[t, cols].astype(f32)
            inputs = (stepw_ref[t, cols] * x).astype(bf16)
            intra = []
            for p in range(cw // LANES):
                piece_in = inputs[:, p * LANES : (p + 1) * LANES]
                got = jnp.zeros((SPAN, LANES), f32)
                for i in range(LANES // size):
                    head = (q * cw + p * LANES) // size + i
                    gap = cum_ref[t, head : head + 1] - cumt_ref[head : head + 1, t]
                    scores = (inner[k] * jnp.exp(jnp.where(causal, gap, -jnp.inf))).astype(bf16)
                    one = jnp.dot(scores, piece_in, preferred_element_type=f32)
                    got = jnp.where(lane == i, one, got)
                intra.append(got)
            there = (before[k][0] * prior[q].astype(f32) + before[k][1]).astype(bf16)
            inter = sum(
                jnp.dot(bc[1, b, t, :], there[b * nb : (b + 1) * nb], preferred_element_type=f32)
                for b in range(S)
            )
            mixed = (
                jnp.concatenate(intra, axis=1) + skip_ref[:, cols] * x
                + jnp.exp(cumw_ref[t, cols]) * inter
            )
            z = z_ref[t, cols].astype(f32)
            gated = mixed * (z / (1.0 + jnp.exp(-z)))
            parts.append(jnp.sum(gated * gated, axis=1, keepdims=True))
            gates[own, t, :] = (gated * gain_ref[:, cols]).astype(bf16)
        summed = summed + jnp.concatenate(parts, axis=0)
        for b in range(1, S):
            gate_x(b, q, own).start()
        for a in range(1, H):
            gate_core(a, 0, q, own).start()
        if q < C - 1:
            weights_step(q)
    here = h * S + s
    squares[here] = jnp.broadcast_to(summed, (tokens, 128)).T[:8]
    for i in range(len(others)):
        square(i, here).start()
    for k in range(min(K, C - 1), C - 1):
        weights_step(k)
    for q in range(K):
        for b in range(1, S):
            gate_x(b, q, block(0, b, q)).wait_recv()
            for a in range(1, H):
                gate_core(a, b, q, block(0, b, q)).start()
    for q in range(K):
        for a in range(1, H):
            for b in range(S):
                gate_core(a, b, q, block(a, b, q)).wait_recv()
    for k in range(C - 1):
        weights_end(k)
    for i, (a, b) in enumerate(others):
        square(i, block(a, b, 0) // K).wait_recv()
    mean = jnp.sum(squares[...], axis=0)[:1] / (S * H * K * cw)
    scale = lax.rsqrt(jnp.broadcast_to(mean + 1e-05, (128, tokens)).T[:, :1])
    total[...] = jnp.zeros_like(total)

    @pl.loop(0, S * H * K)
    def _(blk):
        total[...] += jnp.dot(
            gates[blk], w_all[pl.ds(pl.multiple_of(blk * cw, cw), cw)], preferred_element_type=f32
        )

    o_ref[...] = (total[...] * scale).astype(bf16)
    pl.when(me < C - 1)(lambda: [state(q).wait_send() for q in range(K)] and None)
    for q in range(K):
        for b in range(1, S):
            gate_x(b, q, block(0, 0, q)).wait_send()
        for a in range(1, H):
            for b in range(S):
                gate_core(a, b, q, block(0, b, q)).wait_send()
    for i in range(len(others)):
        square(i, here).wait_send()
    for i in range(3):
        pl.when(me < C - 1)(lambda: rim(i).wait_send())
    for b in range(1, S):
        half_x(b).wait_send()
        half_core(b, h).wait_send()


def finish(axes, *args):
    G, C, S, H = axes
    bf16, f32 = jnp.bfloat16, jnp.float32
    w, x, b = args[:3]
    tokens, width = x.shape
    nb = b.shape[1]
    nstate = nb * S
    cw = min(CHUNK, width)
    K = width // cw
    dma = pltpu.SemaphoreType.DMA
    return pl.pallas_call(
        functools.partial(kernel, axes),
        out_shape=jax.ShapeDtypeStruct((tokens, w.shape[1]), bf16),
        in_specs=[pl.BlockSpec(memory_space=pltpu.VMEM)] * len(args),
        out_specs=pl.BlockSpec(memory_space=pltpu.VMEM),
        scratch_shapes=[
            pltpu.VMEM((C * w.shape[0], w.shape[1]), bf16),
            pltpu.VMEM((K, nstate, cw), bf16),
            pltpu.VMEM((K, nstate, cw), bf16),
            pltpu.VMEM((S * H * K, tokens, cw), bf16),
            pltpu.VMEM((S * H, 8, tokens), f32),
            pltpu.VMEM((tokens, w.shape[1]), f32),
            pltpu.VMEM((RIM, width + 2 * nb), bf16),
            pltpu.VMEM((tokens + RIM, max(width, nb)), f32),
            pltpu.VMEM((tokens, width), bf16),
            pltpu.VMEM((2, S, tokens, nb), bf16),
            pltpu.VMEM((tokens // SPAN, SPAN, SPAN), f32),
            dma((3,)), dma((3,)), dma((S - 1,)), dma((S - 1,)), dma((S - 1,)), dma((S - 1,)),
            dma((C - 1,)), dma((C - 1,)), dma((C - 1,)), dma((C - 1,)),
            dma((2, C - 1, G - 1)), dma((2, C - 1, G - 1)), dma((K,)), dma((K,)),
            dma((S - 1, K)), dma((S - 1, K)), dma((H - 1, S, K)), dma((H - 1, S, K)),
            dma((S * H - 1,)), dma((S * H - 1,)),
        ],
        compiler_params=pltpu.CompilerParams(
            collective_id=0, has_side_effects=True, vmem_limit_bytes=60 * 2**20
        ),
    )(*args)


def local(
    x_in, b_in, c_in, z_in, dt_raw, decay_rate, d_skip, conv_x, conv_b, conv_c, norm_gain, w_out
):
    f32 = jnp.float32
    parts = lax.axis_size("state")
    part = lax.axis_index("state")
    ctx = lax.axis_size("ctx")
    groups = lax.axis_size("groups")
    tokens = x_in.shape[0]
    heads = dt_raw.shape[1] // parts
    width = x_in.shape[1] // parts
    size = width // heads
    spans = tokens // SPAN
    own = lambda a, axis: lax.dynamic_slice_in_dim(
        a, part * (a.shape[axis] // parts), a.shape[axis] // parts, axis
    )
    x_own, dt_own, rate, skip, taps_x = (
        own(x_in, 1), own(dt_raw, 1), own(decay_rate, 0), own(d_skip, 0), own(conv_x, 1)
    )
    step = jax.nn.softplus(dt_own)
    causal = jnp.arange(SPAN)[:, None] >= jnp.arange(SPAN)[None, :]
    cum = jnp.einsum(
        "ts,ksh->kth",
        causal.astype(f32),
        (-rate * step).reshape(spans, SPAN, heads),
        precision=lax.Precision.HIGHEST,
    ).reshape(tokens, heads)
    wide = lambda v: jnp.repeat(v, size, axis=-1)
    return finish(
        (groups, ctx, parts, lax.axis_size("head")),
        w_out,
        x_own,
        b_in,
        c_in,
        z_in,
        wide(step),
        wide(cum),
        cum,
        cum.T,
        wide(skip)[None],
        taps_x,
        conv_b,
        conv_c,
        norm_gain[None],
    )


def solution(mesh):
    return jax.shard_map(
        local,
        mesh=mesh,
        in_specs=(
            P(("groups", "ctx"), "head"),
            P(("groups", "ctx"), "state"),
            P(("groups", "ctx"), "state"),
            P(("groups", "ctx"), ("head", "state")),
            P(("groups", "ctx"), "head"),
            P("head"),
            P("head"),
            P(None, "head"),
            P(None, "state"),
            P(None, "state"),
            P(("head", "state")),
            P("ctx", ("state", "head")),
        ),
        out_specs=P(("groups", "ctx"), ("state", "head")),
        check_vma=False,
    )
```

```python
import functools

import jax
import jax.numpy as jnp
from jax import lax
from jax.experimental import pallas as pl
from jax.experimental.pallas import tpu as pltpu
from jax.sharding import PartitionSpec as P

SPAN = 256
CHUNK = 256
LANES = 128
RIM = 16


def kernel(
    axes, w_ref, x_ref, b_ref, c_ref, z_ref, step_ref, cum_ref, cumt_ref, skip_ref,
    tx_ref, tb_ref, tc_ref, gain_ref, o_ref, w_all, prior, outgoing, gates, squares, total,
    rims, joined, x_conv, bc, inner, stepw_ref, cumw_ref, rim_send, rim_recv, bx_send, bx_recv, bh_send, bh_recv,
    wr_send, wr_recv, wl_send, wl_recv, wy_send, wy_recv, st_send, st_recv,
    gx_send, gx_recv, gc_send, gc_recv, sq_send, sq_recv,
):
    f32, bf16 = jnp.float32, jnp.bfloat16
    G, C, S, H = axes
    g, me, s, h = (lax.axis_index(a) for a in ("groups", "ctx", "state", "head"))
    rows = w_ref.shape[0]
    part = rows // G
    K, nstate, cw = prior.shape
    tokens, nb = c_ref.shape
    width = x_ref.shape[1]
    size = width // cum_ref.shape[1]
    spans = tokens // SPAN
    remote = functools.partial(
        pltpu.make_async_remote_copy, device_id_type=pl.DeviceIdType.MESH
    )

    others = [(a, b) for a in range(H) for b in range(S) if a or b]
    barrier = pltpu.get_barrier_semaphore()

    def greet(to):
        pl.semaphore_signal(barrier, inc=1, device_id=to, device_id_type=pl.DeviceIdType.MESH)

    pl.when(me > 0)(lambda: greet({"ctx": me - 1}))
    pl.when(me < C - 1)(lambda: greet({"ctx": me + 1}))
    for a in range(1, G):
        greet({"groups": lax.rem(g + a, G)})
    for a, b in others:
        greet({"head": lax.rem(h + a, H), "state": lax.rem(s + b, S)})
    peers = G - 1 + len(others) + (me > 0).astype(jnp.int32) + (me < C - 1).astype(jnp.int32)
    pl.semaphore_wait(barrier, peers)

    def piece(j, half):
        return w_all.at[pl.ds(pl.multiple_of(j * rows + half * part, part), part)]

    def right(k, j):
        return remote(piece(j, g), piece(j, g), wr_send.at[k], wr_recv.at[k], device_id={"ctx": me + 1})

    def left(k, j):
        return remote(piece(j, g), piece(j, g), wl_send.at[k], wl_recv.at[k], device_id={"ctx": me - 1})

    def across(way, k, a, j, half):
        return remote(
            piece(j, half), piece(j, half), wy_send.at[way, k, a - 1], wy_recv.at[way, k, a - 1],
            device_id={"groups": lax.rem(g + a, G)},
        )

    def weights_step(k):
        @pl.when(me - 1 - k >= 0)
        def _():
            right(k, me - 1 - k).wait_recv()
            for a in range(1, G):
                across(0, k, a, me - 1 - k, g).start()
            if k + 1 <= C - 2:
                pl.when(me < C - 1)(lambda: right(k + 1, me - 1 - k).start())

        @pl.when(me + 1 + k <= C - 1)
        def _():
            left(k, me + 1 + k).wait_recv()
            for a in range(1, G):
                across(1, k, a, me + 1 + k, g).start()
            if k + 1 <= C - 2:
                pl.when(me > 0)(lambda: left(k + 1, me + 1 + k).start())

    def weights_end(k):
        @pl.when((me - k >= 0) & (me < C - 1))
        def _():
            right(k, me - k).wait_send()

        @pl.when((me + k <= C - 1) & (me > 0))
        def _():
            left(k, me + k).wait_send()

        for way, j, there in ((0, me - 1 - k, me - 1 - k >= 0), (1, me + 1 + k, me + 1 + k <= C - 1)):
            @pl.when(there)
            def _():
                for a in range(1, G):
                    across(way, k, a, j, g).wait_send()
                    across(way, k, a, j, lax.rem(g - a + G, G)).wait_recv()

    def state(q):
        return remote(
            outgoing.at[q], prior.at[q], st_send.at[q], st_recv.at[q], device_id={"ctx": me + 1}
        )

    def block(a, b, q):
        return (lax.rem(h + H - a, H) * S + lax.rem(s + S - b, S)) * K + q

    def gate_x(b, q, blk):
        return remote(
            gates.at[blk], gates.at[blk], gx_send.at[b - 1, q], gx_recv.at[b - 1, q],
            device_id={"state": lax.rem(s + b, S)},
        )

    def gate_core(a, b, q, blk):
        return remote(
            gates.at[blk], gates.at[blk], gc_send.at[a - 1, b, q], gc_recv.at[a - 1, b, q],
            device_id={"head": lax.rem(h + a, H)},
        )

    def square(i, slot):
        a, b = others[i]
        return remote(
            squares.at[slot], squares.at[slot], sq_send.at[i], sq_recv.at[i],
            device_id={"head": lax.rem(h + a, H), "state": lax.rem(s + b, S)},
        )

    def rim(i):
        ref, at = ((x_ref, 0), (b_ref, width), (c_ref, width + nb))[i]
        return remote(
            ref.at[pl.ds(tokens - RIM, RIM)], rims.at[:, pl.ds(at, ref.shape[1])],
            rim_send.at[i], rim_recv.at[i], device_id={"ctx": me + 1},
        )

    def half_x(b):
        return remote(
            bc.at[h, s], bc.at[h, s], bx_send.at[b - 1], bx_recv.at[b - 1],
            device_id={"state": lax.rem(s + b, S)},
        )

    def half_core(b, which):
        there = lax.rem(s + S - b, S)
        return remote(
            bc.at[which, there], bc.at[which, there], bh_send.at[b - 1], bh_recv.at[b - 1],
            device_id={"head": 1 - h},
        )

    for i in range(3):
        pl.when(me < C - 1)(lambda: rim(i).start())
    w_all[pl.ds(pl.multiple_of(me * rows, rows), rows)] = w_ref[...]

    pl.when(me < C - 1)(lambda: right(0, me).start())
    pl.when(me > 0)(lambda: left(0, me).start())

    @pl.when(me == 0)
    def _():
        prior[...] = jnp.zeros_like(prior)
        rims[...] = jnp.zeros_like(rims)

    heads = cum_ref.shape[1]
    spread = (
        lax.broadcasted_iota(jnp.int32, (heads, width), 1) // size
        == lax.broadcasted_iota(jnp.int32, (heads, width), 0)
    ).astype(f32)
    for small, large in ((step_ref, stepw_ref), (cum_ref, cumw_ref)):
        large[...] = jnp.dot(
            small[...], spread, precision=lax.Precision.HIGHEST, preferred_element_type=f32
        )
    for i in range(3):
        pl.when(me > 0)(lambda: rim(i).wait_recv())

    def conv(ref, taps_ref, at):
        wide = ref.shape[1]
        joined[:RIM, :wide] = rims[:, at : at + wide].astype(f32)
        joined[RIM:, :wide] = ref[...].astype(f32)
        taps = taps_ref.shape[0]
        v = jnp.zeros((tokens, wide), f32)
        for k in range(taps):
            v = v + taps_ref[k : k + 1, :] * joined[pl.ds(RIM - taps + 1 + k, tokens), :wide]
        return (v / (1.0 + jnp.exp(-v))).astype(bf16)

    bc[0, s] = conv(b_ref, tb_ref, width)
    bc[1, s] = conv(c_ref, tc_ref, width + nb)
    for b in range(1, S):
        half_x(b).start()
    x_conv[...] = conv(x_ref, tx_ref, 0)
    for b in range(1, S):
        half_x(b).wait_recv()
        half_core(b, h).start()
    weights_step(0)
    for b in range(1, S):
        half_core(b, 1 - h).wait_recv()
    causal = lax.broadcasted_iota(jnp.int32, (SPAN, SPAN), 0) >= lax.broadcasted_iota(
        jnp.int32, (SPAN, SPAN), 1
    )
    lane = lax.broadcasted_iota(jnp.int32, (SPAN, LANES), 1) // size
    for k in range(spans):
        t = slice(k * SPAN, (k + 1) * SPAN)
        inner[k] = sum(
            lax.dot_general(
                bc[1, b, t, :], bc[0, b, t, :], (((1,), (1,)), ((), ())), preferred_element_type=f32
            )
            for b in range(S)
        )

    def pass_on(q):
        for b in range(1, S):
            gate_x(b, q, block(0, b, q)).wait_recv()
            for a in range(1, H):
                gate_core(a, b, q, block(0, b, q)).start()

    summed = jnp.zeros((tokens, 1), f32)
    for q in range(K):
        cols = slice(q * cw, (q + 1) * cw)
        running = jnp.zeros((nstate, cw), f32)
        reach = jnp.ones((1, cw), f32)
        before = []
        for k in range(spans):
            t = slice(k * SPAN, (k + 1) * SPAN)
            before.append((reach, running))
            last = cumw_ref[(k + 1) * SPAN - 1 : (k + 1) * SPAN, cols]
            weighted = (
                jnp.exp(last - cumw_ref[t, cols]) * stepw_ref[t, cols] * x_conv[t, cols].astype(f32)
            ).astype(bf16)
            update = jnp.concatenate(
                [
                    lax.dot_general(
                        bc[0, b, t, :], weighted, (((0,), (0,)), ((), ())), preferred_element_type=f32
                    )
                    for b in range(S)
                ],
                axis=0,
            )
            decay = jnp.exp(last)
            running = decay * running + update
            reach = reach * decay
        pl.when(me > 0)(lambda: state(q).wait_recv())

        @pl.when(me < C - 1)
        def _():
            outgoing[q] = (reach * prior[q].astype(f32) + running).astype(bf16)
            state(q).start()

        own = block(0, 0, q)
        parts = []
        for k in range(spans):
            t = slice(k * SPAN, (k + 1) * SPAN)
            x = x_conv[t, cols].astype(f32)
            inputs = (stepw_ref[t, cols] * x).astype(bf16)
            intra = []
            for p in range(cw // LANES):
                piece_in = inputs[:, p * LANES : (p + 1) * LANES]
                got = jnp.zeros((SPAN, LANES), f32)
                for i in range(LANES // size):
                    head = (q * cw + p * LANES) // size + i
                    gap = cum_ref[t, head : head + 1] - cumt_ref[head : head + 1, t]
                    scores = (inner[k] * jnp.exp(jnp.where(causal, gap, -jnp.inf))).astype(bf16)
                    one = jnp.dot(scores, piece_in, preferred_element_type=f32)
                    got = jnp.where(lane == i, one, got)
                intra.append(got)
            there = (before[k][0] * prior[q].astype(f32) + before[k][1]).astype(bf16)
            inter = sum(
                jnp.dot(bc[1, b, t, :], there[b * nb : (b + 1) * nb], preferred_element_type=f32)
                for b in range(S)
            )
            mixed = (
                jnp.concatenate(intra, axis=1) + skip_ref[:, cols] * x
                + jnp.exp(cumw_ref[t, cols]) * inter
            )
            z = z_ref[t, cols].astype(f32)
            gated = mixed * (z / (1.0 + jnp.exp(-z)))
            parts.append(jnp.sum(gated * gated, axis=1, keepdims=True))
            gates[own, t, :] = (gated * gain_ref[:, cols]).astype(bf16)
        summed = summed + jnp.concatenate(parts, axis=0)
        for b in range(1, S):
            gate_x(b, q, own).start()
        for a in range(1, H):
            gate_core(a, 0, q, own).start()
        if q + 1 < C - 1:
            weights_step(q + 1)
        if q >= 1:
            pass_on(q - 1)
    here = h * S + s
    squares[here] = jnp.broadcast_to(summed, (tokens, 128)).T[:8]
    for i in range(len(others)):
        square(i, here).start()
    for k in range(min(K + 1, C - 1), C - 1):
        weights_step(k)
    for k in range(C - 1):
        weights_end(k)
    tile = min(256, total.shape[1])
    for q in range(K):
        if q == max(K - 2, 0):
            pass_on(K - 1)
        for a in range(1, H):
            for b in range(S):
                gate_core(a, b, q, block(a, b, q)).wait_recv()

        @pl.loop(0, total.shape[1] // tile)
        def _(n):
            cols = pl.ds(pl.multiple_of(n * tile, tile), tile)
            acc = jnp.zeros((tokens, tile), f32) if q == 0 else total[:, cols]
            for d in range(S * H):
                blk = d * K + q
                acc = acc + jnp.dot(
                    gates[blk], w_all[blk * cw : (blk + 1) * cw, cols], preferred_element_type=f32
                )
            total[:, cols] = acc

    for i, (a, b) in enumerate(others):
        square(i, block(a, b, 0) // K).wait_recv()
    mean = jnp.sum(squares[...], axis=0)[:1] / (S * H * K * cw)
    scale = lax.rsqrt(jnp.broadcast_to(mean + 1e-05, (128, tokens)).T[:, :1])
    o_ref[...] = (total[...] * scale).astype(bf16)
    pl.when(me < C - 1)(lambda: [state(q).wait_send() for q in range(K)] and None)
    for q in range(K):
        for b in range(1, S):
            gate_x(b, q, block(0, 0, q)).wait_send()
        for a in range(1, H):
            for b in range(S):
                gate_core(a, b, q, block(0, b, q)).wait_send()
    for i in range(len(others)):
        square(i, here).wait_send()
    for i in range(3):
        pl.when(me < C - 1)(lambda: rim(i).wait_send())
    for b in range(1, S):
        half_x(b).wait_send()
        half_core(b, h).wait_send()


def finish(axes, *args):
    G, C, S, H = axes
    bf16, f32 = jnp.bfloat16, jnp.float32
    w, x, b = args[:3]
    tokens, width = x.shape
    nb = b.shape[1]
    nstate = nb * S
    cw = min(CHUNK, width)
    K = width // cw
    dma = pltpu.SemaphoreType.DMA
    return pl.pallas_call(
        functools.partial(kernel, axes),
        out_shape=jax.ShapeDtypeStruct((tokens, w.shape[1]), bf16),
        in_specs=[pl.BlockSpec(memory_space=pltpu.VMEM)] * len(args),
        out_specs=pl.BlockSpec(memory_space=pltpu.VMEM),
        scratch_shapes=[
            pltpu.VMEM((C * w.shape[0], w.shape[1]), bf16),
            pltpu.VMEM((K, nstate, cw), bf16),
            pltpu.VMEM((K, nstate, cw), bf16),
            pltpu.VMEM((S * H * K, tokens, cw), bf16),
            pltpu.VMEM((S * H, 8, tokens), f32),
            pltpu.VMEM((tokens, w.shape[1]), f32),
            pltpu.VMEM((RIM, width + 2 * nb), bf16),
            pltpu.VMEM((tokens + RIM, max(width, nb)), f32),
            pltpu.VMEM((tokens, width), bf16),
            pltpu.VMEM((2, S, tokens, nb), bf16),
            pltpu.VMEM((tokens // SPAN, SPAN, SPAN), f32),
            pltpu.VMEM((tokens, width), f32),
            pltpu.VMEM((tokens, width), f32),
            dma((3,)), dma((3,)), dma((S - 1,)), dma((S - 1,)), dma((S - 1,)), dma((S - 1,)),
            dma((C - 1,)), dma((C - 1,)), dma((C - 1,)), dma((C - 1,)),
            dma((2, C - 1, G - 1)), dma((2, C - 1, G - 1)), dma((K,)), dma((K,)),
            dma((S - 1, K)), dma((S - 1, K)), dma((H - 1, S, K)), dma((H - 1, S, K)),
            dma((S * H - 1,)), dma((S * H - 1,)),
        ],
        compiler_params=pltpu.CompilerParams(
            collective_id=0, has_side_effects=True, vmem_limit_bytes=60 * 2**20
        ),
    )(*args)


def local(
    x_in, b_in, c_in, z_in, dt_raw, decay_rate, d_skip, conv_x, conv_b, conv_c, norm_gain, w_out
):
    f32 = jnp.float32
    parts = lax.axis_size("state")
    part = lax.axis_index("state")
    ctx = lax.axis_size("ctx")
    groups = lax.axis_size("groups")
    tokens = x_in.shape[0]
    heads = dt_raw.shape[1] // parts
    width = x_in.shape[1] // parts
    size = width // heads
    spans = tokens // SPAN
    own = lambda a, axis: lax.dynamic_slice_in_dim(
        a, part * (a.shape[axis] // parts), a.shape[axis] // parts, axis
    )
    x_own, dt_own, rate, skip, taps_x = (
        own(x_in, 1), own(dt_raw, 1), own(decay_rate, 0), own(d_skip, 0), own(conv_x, 1)
    )
    step = jax.nn.softplus(dt_own)
    causal = jnp.arange(SPAN)[:, None] >= jnp.arange(SPAN)[None, :]
    cum = jnp.einsum(
        "ts,ksh->kth",
        causal.astype(f32),
        (-rate * step).reshape(spans, SPAN, heads),
        precision=lax.Precision.HIGHEST,
    ).reshape(tokens, heads)
    wide = lambda v: jnp.repeat(v, size, axis=-1)
    return finish(
        (groups, ctx, parts, lax.axis_size("head")),
        w_out,
        x_own,
        b_in,
        c_in,
        z_in,
        step,
        cum,
        cum.T,
        wide(skip)[None],
        taps_x,
        conv_b,
        conv_c,
        norm_gain[None],
    )


def solution(mesh):
    return jax.shard_map(
        local,
        mesh=mesh,
        in_specs=(
            P(("groups", "ctx"), "head"),
            P(("groups", "ctx"), "state"),
            P(("groups", "ctx"), "state"),
            P(("groups", "ctx"), ("head", "state")),
            P(("groups", "ctx"), "head"),
            P("head"),
            P("head"),
            P(None, "head"),
            P(None, "state"),
            P(None, "state"),
            P(("head", "state")),
            P("ctx", ("state", "head")),
        ),
        out_specs=P(("groups", "ctx"), ("state", "head")),
        check_vma=False,
    )
```
